32 devices in a mesh: row: 4 (over y, x), col: 8 (over z, core).
Axes of the slice: x: 2, y: 2, z: 4, core: 2. Of those that a mesh axis runs over, the one named last changes fastest.
Arguments:
- value: bfloat16 [1024, 1024, 128], P('row', 'col'), may hold values from -6 to 6
- gate: bfloat16 [1024, 1024, 128], P('row', 'col'), may hold values from -6 to 6
- filter_real: float32 [1024, 1024, 128], P(None, ('row', 'col')), may hold values from -6 to 6
- filter_imag: float32 [1024, 1024, 128], P(None, ('row', 'col')), may hold values from -6 to 6
- skip: float32 [128], replicated, may hold values from -4 to 4
Outputs:
- gated: bfloat16 [1024, 1024, 128], P('row', 'col')
The draws below stay inside these ranges and needn't reach their ends.
All inputs are finite; a program needn't handle non-finite values.
Results may differ from the reference program's by a relative error of at most 0.001.
Values may be sent and summed in bfloat16 or wider, within the bound.
A program may use at most 192 MiB of HBM per device.

```python
import math
import jax
import jax.numpy as jnp
from jax import lax

GRID_P = 1024
GRID_Q = 1024
CH = 128


def steps_of(rng, dims, shards, low, largest):
    def one(position, shards_of):
        steps = jax.random.uniform(jax.random.fold_in(jax.random.fold_in(rng, 6), position), (shards_of,), jnp.float32, low / len(shards), largest / len(shards))
        return jnp.repeat(jnp.exp(steps), dims[position] // shards_of).reshape((-1,) + (1,) * (len(dims) - position - 1))

    factor_of = one(*shards[0])
    for cut in shards[1:]:
        factor_of = factor_of * one(*cut)
    return factor_of


def normal_values(key, extent, scale, bound, shards=(), kind=jnp.bfloat16):
    entries = scale * jax.random.normal(key, extent, jnp.float32)
    if shards:
        entries = entries * steps_of(key, extent, shards, -0.22, 0.18)
    return jnp.clip(entries, -bound, bound).astype(kind)


def setup_inputs(seed: int = 0) -> dict:
    key_list = jax.random.split(jax.random.key(seed), 6)
    return {
        "value": normal_values(key_list[0], (GRID_P, GRID_Q, CH), 1.0, 6.0, ((0, 4), (1, 8))),
        "gate": normal_values(key_list[1], (GRID_P, GRID_Q, CH), 1.0, 6.0, ((0, 4), (1, 8))),
        "filter_real": normal_values(key_list[2], (GRID_Q, GRID_P, CH), 1.0, 6.0, ((1, 32),), jnp.float32),
        "filter_imag": normal_values(key_list[3], (GRID_Q, GRID_P, CH), 1.0, 6.0, ((1, 32),), jnp.float32),
        "skip": normal_values(key_list[4], (CH,), 1.0, 4.0, (), jnp.float32),
    }


def reference(value, gate, filter_real, filter_imag, skip):
    positions = GRID_P * GRID_Q
    block_size = math.gcd(CH, 16)
    groups = CH // block_size
    flat_value = value.reshape(positions, CH)
    flat_gate = gate.reshape(positions, CH)
    flat_real = filter_real.reshape(positions, CH)
    flat_imag = filter_imag.reshape(positions, CH)

    def one_block(group_index):
        first_channel = (group_index * block_size).astype(jnp.int32)
        part_value = lax.dynamic_slice_in_dim(flat_value, first_channel, block_size, 1).astype(jnp.float32)
        part_gate = lax.dynamic_slice_in_dim(flat_gate, first_channel, block_size, 1).astype(jnp.float32)
        part_real = lax.dynamic_slice_in_dim(flat_real, first_channel, block_size, 1)
        part_imag = lax.dynamic_slice_in_dim(flat_imag, first_channel, block_size, 1)
        part_skip = lax.dynamic_slice_in_dim(skip, first_channel, block_size, 0)
        spectrum = jnp.fft.fft(part_value, axis=0)
        response = lax.complex(part_real, part_imag)
        convolved = jnp.real(jnp.fft.ifft(spectrum * response, axis=0))
        result = part_gate * (convolved + part_skip * part_value)
        return result.astype(jnp.bfloat16)

    blocks = lax.map(one_block, jnp.arange(groups, dtype=jnp.int32))
    return jnp.moveaxis(blocks, 0, 1).reshape(GRID_P, GRID_Q, CH)
```

```python
import math

import jax
import jax.numpy as jnp
from jax import lax
from jax.sharding import PartitionSpec as P

full_turn = 2.0 * math.pi
code_top = 250.0
chunk_count = 2


def phase_table(left, right, period):
    angles = (left * right % period).astype(jnp.float32) * (full_turn / period)
    return jnp.cos(angles), jnp.sin(angles)


def contract(spec, left, right):
    return jnp.einsum(
        spec, left, right, precision=lax.Precision.HIGH, preferred_element_type=jnp.float32
    )


def encode(array, largest):
    scaled = array * (code_top / largest)
    return (scaled * jnp.abs(scaled)).astype(jnp.float16)


def decode(coded, largest):
    wide = coded.astype(jnp.float32)
    root = jnp.sqrt(jnp.abs(wide)) * (largest * (1.0 / code_top))
    return jnp.where(wide < 0.0, -root, root)


def bound_of(array):
    return jnp.maximum(jnp.max(jnp.abs(array)).astype(jnp.float32), 1e-30)


def convolve(value, gate, filter_real, filter_imag, skip):
    row_count = lax.axis_size("row")
    col_count = lax.axis_size("col")
    both = ("row", "col")
    local_rows, local_cols, channels = value.shape
    grid_rows = local_rows * row_count
    grid_cols = local_cols * col_count
    narrow = local_cols // row_count
    devices = row_count * col_count
    local_freq = grid_rows // devices
    period = grid_rows * grid_cols
    width = narrow // chunk_count
    row_index = lax.axis_index("row")
    col_index = lax.axis_index("col")

    freq = jnp.arange(grid_rows, dtype=jnp.int32)
    cosine, sine = phase_table(freq[:, None], freq[None, :], grid_rows)
    col_matrix = jnp.stack(
        [
            cosine.reshape(devices, local_freq, grid_rows),
            -sine.reshape(devices, local_freq, grid_rows),
        ],
        axis=1,
    )

    pieces = value.reshape(local_rows, row_count, chunk_count, width, channels)
    columns = []
    for chunk in range(chunk_count):
        part = lax.all_to_all(
            pieces[:, :, chunk], "row", split_axis=1, concat_axis=0, tiled=True
        )
        columns.append(part.reshape(grid_rows, width, channels))

    kq = jnp.arange(grid_cols, dtype=jnp.int32)

    def row_matrix(chunk):
        source = jnp.arange(devices, dtype=jnp.int32)
        base = source % col_count * local_cols + source // col_count * narrow + chunk * width
        position = base[:, None] + jnp.arange(width, dtype=jnp.int32)[None, :]
        c, s = phase_table(kq[:, None, None], position[None], grid_cols)
        return jnp.stack([jnp.stack([c, s], axis=2), jnp.stack([-s, c], axis=2)])

    twists = []
    for chunk in range(chunk_count):
        position = (
            col_index * local_cols
            + row_index * narrow
            + chunk * width
            + jnp.arange(width, dtype=jnp.int32)
        )
        c, s = phase_table(freq[:, None], position[None, :], period)
        c = c.reshape(devices, local_freq, width).transpose(0, 2, 1)[..., None]
        s = s.reshape(devices, local_freq, width).transpose(0, 2, 1)[..., None]
        twists.append((c, s))

    row_parts = [row_matrix(chunk) for chunk in range(chunk_count)]
    frequencies = None
    for chunk in range(chunk_count):
        spectrum = contract("diap,pwz->diwaz", col_matrix, columns[chunk].astype(jnp.float32))
        c, s = twists[chunk]
        real, imag = spectrum[:, 0], spectrum[:, 1]
        spectrum = jnp.stack([real * c + imag * s, imag * c - real * s], axis=1)
        largest = bound_of(columns[chunk]) * float(grid_rows)
        every = lax.all_gather(largest, both)
        arrived = lax.all_to_all(encode(spectrum, largest), both, 0, 0, tiled=True)
        arrived = decode(arrived, every[:, None, None, None, None])
        term = contract("oksiw,siwaz->okaz", row_parts[chunk], arrived)
        frequencies = term if frequencies is None else frequencies + term

    real, imag = frequencies[0], frequencies[1]
    filtered = jnp.stack(
        [
            real * filter_real - imag * filter_imag,
            real * filter_imag + imag * filter_real,
        ]
    )

    settled = []
    for chunk in range(chunk_count):
        leaving = contract("oksiw,okaz->siwaz", row_parts[chunk], filtered)
        largest = bound_of(leaving)
        every = lax.all_gather(largest, both)
        returned = lax.all_to_all(encode(leaving, largest), both, 0, 0, tiled=True)
        returned = decode(returned, every[:, None, None, None, None] * (1.0 / period))
        c, s = twists[chunk]
        real, imag = returned[:, 0], returned[:, 1]
        returned = jnp.stack([real * c - imag * s, imag * c + real * s], axis=1)
        convolved = contract("diap,diwaz->pwz", col_matrix, returned)
        largest = bound_of(convolved)
        every = lax.all_gather(largest, "row")
        coded = encode(convolved, largest).reshape(row_count, local_rows, width, channels)
        coded = lax.all_to_all(coded, "row", 0, 0, tiled=True)
        settled.append(decode(coded, every[:, None, None, None]))
    settled = jnp.stack(settled, axis=1)
    settled = settled.transpose(2, 0, 1, 3, 4).reshape(local_rows, local_cols, channels)
    result = gate.astype(jnp.float32) * (settled + skip * value.astype(jnp.float32))
    return result.astype(jnp.bfloat16)


def solution(mesh):
    return jax.shard_map(
        convolve,
        mesh=mesh,
        in_specs=(
            P("row", "col", None),
            P("row", "col", None),
            P(None, ("row", "col"), None),
            P(None, ("row", "col"), None),
            P(),
        ),
        out_specs=P("row", "col", None),
        check_vma=False,
    )
```

```python
import math

import jax
import jax.numpy as jnp
from jax import lax
from jax.sharding import PartitionSpec as P

full_turn = 2.0 * math.pi
code_top = 250.0
chunk_count = 2


def phase_table(left, right, period):
    angles = (left * right % period).astype(jnp.float32) * (full_turn / period)
    return jnp.cos(angles), jnp.sin(angles)


def contract(spec, left, right):
    return jnp.einsum(
        spec, left, right, precision=lax.Precision.HIGH, preferred_element_type=jnp.float32
    )


def encode(array, largest):
    scaled = array * (code_top / largest)
    return (scaled * jnp.abs(scaled)).astype(jnp.float16)


def decode(coded, largest):
    wide = coded.astype(jnp.float32)
    root = jnp.sqrt(jnp.abs(wide)) * (largest * (1.0 / code_top))
    return jnp.where(wide < 0.0, -root, root)


def bound_of(array):
    return jnp.maximum(jnp.max(jnp.abs(array)).astype(jnp.float32), 1e-30)


def convolve(value, gate, filter_real, filter_imag, skip):
    row_count = lax.axis_size("row")
    col_count = lax.axis_size("col")
    both = ("row", "col")
    local_rows, local_cols, channels = value.shape
    grid_rows = local_rows * row_count
    grid_cols = local_cols * col_count
    narrow = local_cols // row_count
    devices = row_count * col_count
    local_freq = grid_rows // devices
    period = grid_rows * grid_cols
    width = narrow // chunk_count
    row_index = lax.axis_index("row")
    col_index = lax.axis_index("col")

    freq = jnp.arange(grid_rows, dtype=jnp.int32)
    cosine, sine = phase_table(freq[:, None], freq[None, :], grid_rows)
    col_matrix = jnp.stack(
        [
            cosine.reshape(devices, local_freq, grid_rows),
            -sine.reshape(devices, local_freq, grid_rows),
        ],
        axis=1,
    )

    pieces = value.reshape(local_rows, row_count, chunk_count, width, channels)
    columns = []
    for chunk in range(chunk_count):
        part = lax.all_to_all(
            pieces[:, :, chunk], "row", split_axis=1, concat_axis=0, tiled=True
        )
        columns.append(part.reshape(grid_rows, width, channels))

    kq = jnp.arange(grid_cols, dtype=jnp.int32)

    def row_matrix(chunk):
        source = jnp.arange(devices, dtype=jnp.int32)
        base = source % col_count * local_cols + source // col_count * narrow + chunk * width
        position = base[:, None] + jnp.arange(width, dtype=jnp.int32)[None, :]
        c, s = phase_table(kq[:, None, None], position[None], grid_cols)
        return jnp.stack([jnp.stack([c, s], axis=2), jnp.stack([-s, c], axis=2)])

    twists = []
    for chunk in range(chunk_count):
        position = (
            col_index * local_cols
            + row_index * narrow
            + chunk * width
            + jnp.arange(width, dtype=jnp.int32)
        )
        c, s = phase_table(freq[:, None], position[None, :], period)
        c = c.reshape(devices, local_freq, width).transpose(0, 2, 1)[..., None]
        s = s.reshape(devices, local_freq, width).transpose(0, 2, 1)[..., None]
        twists.append((c, s))

    row_parts = [row_matrix(chunk) for chunk in range(chunk_count)]
    first_top = lax.pmax(bound_of(value), both) * float(grid_rows)
    frequencies = None
    for chunk in range(chunk_count):
        spectrum = contract("diap,pwz->diwaz", col_matrix, columns[chunk].astype(jnp.float32))
        c, s = twists[chunk]
        real, imag = spectrum[:, 0], spectrum[:, 1]
        spectrum = jnp.stack([real * c + imag * s, imag * c - real * s], axis=1)
        arrived = lax.all_to_all(encode(spectrum, first_top), both, 0, 0, tiled=True)
        arrived = decode(arrived, first_top)
        term = contract("oksiw,siwaz->okaz", row_parts[chunk], arrived)
        frequencies = term if frequencies is None else frequencies + term

    real, imag = frequencies[0], frequencies[1]
    filtered = jnp.stack(
        [
            real * filter_real - imag * filter_imag,
            real * filter_imag + imag * filter_real,
        ]
    )

    largest = bound_of(filtered)
    norms = jnp.sum(jnp.square(filtered * (1.0 / largest)), axis=(0, 1))
    second_top = lax.pmax(largest * jnp.sqrt(jnp.max(norms) * grid_cols), both)
    second_top = jnp.maximum(second_top, 1e-30)
    last_top = second_top * (float(grid_rows) / period)
    settled = []
    for chunk in range(chunk_count):
        leaving = contract("oksiw,okaz->siwaz", row_parts[chunk], filtered)
        returned = lax.all_to_all(encode(leaving, second_top), both, 0, 0, tiled=True)
        returned = decode(returned, second_top * (1.0 / period))
        c, s = twists[chunk]
        real, imag = returned[:, 0], returned[:, 1]
        returned = jnp.stack([real * c - imag * s, imag * c + real * s], axis=1)
        convolved = contract("diap,diwaz->pwz", col_matrix, returned)
        coded = encode(convolved, last_top).reshape(row_count, local_rows, width, channels)
        coded = lax.all_to_all(coded, "row", 0, 0, tiled=True)
        settled.append(decode(coded, last_top))
    settled = jnp.stack(settled, axis=1)
    settled = settled.transpose(2, 0, 1, 3, 4).reshape(local_rows, local_cols, channels)
    result = gate.astype(jnp.float32) * (settled + skip * value.astype(jnp.float32))
    return result.astype(jnp.bfloat16)


def solution(mesh):
    return jax.shard_map(
        convolve,
        mesh=mesh,
        in_specs=(
            P("row", "col", None),
            P("row", "col", None),
            P(None, ("row", "col"), None),
            P(None, ("row", "col"), None),
            P(),
        ),
        out_specs=P("row", "col", None),
        check_vma=False,
    )
```
